256 devices in a mesh: dp: 32 (over z, x), tensor: 8 (over y, core).
Axes of the slice: x: 4, y: 4, z: 8, core: 2. Of those that a mesh axis runs over, the one named last changes fastest.
Arguments:
- activations: bfloat16 [16384, 128, 128], P('dp', 'tensor'), may hold values from -6 to 6
- cotangent: bfloat16 [16384, 128, 128], P('dp', 'tensor'), may hold values from -0.004119873 to 0.004119873
- left_factor: bfloat16 [128, 128], replicated, may hold values from -0.5 to 0.5
- right_factor: bfloat16 [128, 128], replicated, may hold values from -0.5 to 0.5
- scale_power: int32 [128, 128], replicated, may hold values from -5 to -3
- grid_bits: int32 [128, 128], replicated, may hold values from 4 to 7
Outputs:
- grad_left: float32 [128, 128], replicated
- grad_right: float32 [128, 128], replicated
The draws below stay inside these ranges and needn't reach their ends.
All inputs are finite; a program needn't handle non-finite values.
Results may differ from the reference program's by a relative error of at most 0.009.
The reference program's roundings to bfloat16 on the way (of `rotated`, `grad_mid` and `grad_rot`) count: a program that leaves them out, or rounds other values in their place, can miss the bound.
Values may be sent and summed in bfloat16 or wider, within the bound.
No kernel may reach another device: no remote copies, remote signals or barrier semaphores. Data moves between devices by JAX's collectives and lax.ppermute only.
A program may use at most 64 MiB of HBM per device.

```python
import jax
import jax.numpy as jnp
from jax import lax

LEFT = 128
RIGHT = 128
TOK_DEV = 512
TOKENS = 16384


def set_ends(entries, rng, smallest, top_value):
    extent = entries.shape
    place = [jax.random.randint(jax.random.fold_in(rng, axis), (), 0, extent[axis]) for axis in range(len(extent))]
    entries = entries.at[tuple(place)].set(smallest)
    longest = extent.index(max(extent))
    place[longest] = (place[longest] + 1) % extent[longest]
    return entries.at[tuple(place)].set(top_value)


def shard_levels(key, dims, shards, smallest, high):
    def one(axis_at, blocks):
        draws = jax.random.uniform(jax.random.fold_in(jax.random.fold_in(key, 6), axis_at), (blocks,), jnp.float32, smallest / len(shards), high / len(shards))
        return jnp.repeat(jnp.exp(draws), dims[axis_at] // blocks).reshape((-1,) + (1,) * (len(dims) - axis_at - 1))

    gain = one(*shards[0])
    for cut in shards[1:]:
        gain = gain * one(*cut)
    return gain


def bell_draw(key, dims, spread, bound, shards=(), kind=jnp.bfloat16):
    factor_of = shard_levels(key, dims, shards, -0.22, 0.18) if shards else 1.0
    array = jax.random.normal(key, dims, jnp.float32) * spread * factor_of
    return jnp.minimum(jnp.maximum(array, -bound), bound).astype(kind)


def setup_inputs(seed: int = 0) -> dict:
    key_list = jax.random.split(jax.random.key(seed), 7)
    activations = bell_draw(key_list[0], (TOKENS, LEFT, RIGHT), 1.0, 6.0, ((0, 32), (1, 8)))
    cotangent = bell_draw(key_list[1], (TOKENS, LEFT, RIGHT), (1.0 / (TOKENS * RIGHT) ** 0.5), 0.004119873, ((0, 32), (1, 8)))
    left_factor = bell_draw(key_list[2], (LEFT, LEFT), LEFT ** -0.5, 0.5)
    right_factor = bell_draw(key_list[3], (RIGHT, RIGHT), RIGHT ** -0.5, 0.5)
    scale_power = set_ends(jax.random.randint(key_list[4], (LEFT, RIGHT), -5, -2), jax.random.fold_in(key_list[4], 1), -5, (-2) - 1).astype(jnp.int32)
    grid_bits = set_ends(jax.random.randint(key_list[5], (LEFT, RIGHT), 4, 8), jax.random.fold_in(key_list[5], 1), 4, 7).astype(jnp.int32)
    return dict(activations=activations, cotangent=cotangent, left_factor=left_factor, right_factor=right_factor, scale_power=scale_power, grid_bits=grid_bits)


def block_grads(carry, pieces, left_factor, right_factor, lower_edge, upper_edge):
    acts, cot = pieces
    rotated = jnp.einsum('tij,jb->tib', acts.astype(jnp.float32), right_factor.astype(jnp.float32)).astype(jnp.bfloat16)
    transformed = jnp.einsum('ia,tib->tab', left_factor.astype(jnp.float32), rotated.astype(jnp.float32))
    inside = (transformed >= lower_edge) & (transformed <= upper_edge)
    grad_mid = jnp.where(inside, cot.astype(jnp.float32), jnp.float32(0.0)).astype(jnp.bfloat16)
    grad_rot = jnp.einsum('ia,tab->tib', left_factor.astype(jnp.float32), grad_mid.astype(jnp.float32)).astype(jnp.bfloat16)
    part_left = jnp.einsum('tib,tab->ia', rotated.astype(jnp.float32), grad_mid.astype(jnp.float32))
    part_right = jnp.einsum('tij,tib->jb', acts.astype(jnp.float32), grad_rot.astype(jnp.float32))
    return (carry[0] + part_left, carry[1] + part_right), None


def reference(activations, cotangent, left_factor, right_factor, scale_power, grid_bits):
    step_size = jnp.exp2(scale_power.astype(jnp.float32))
    half_grid = jnp.exp2((grid_bits - 1).astype(jnp.float32))
    lower_edge = -half_grid * step_size
    upper_edge = (half_grid - 1.0) * step_size
    blocks = activations.shape[0] // TOK_DEV
    acts = activations.reshape(blocks, TOK_DEV, LEFT, RIGHT)
    cots = cotangent.reshape(blocks, TOK_DEV, LEFT, RIGHT)
    start = (jnp.zeros((LEFT, LEFT), jnp.float32), jnp.zeros((RIGHT, RIGHT), jnp.float32))

    def scan_body(carry, pieces):
        return block_grads(carry, pieces, left_factor, right_factor, lower_edge, upper_edge)

    totals, unused = lax.scan(scan_body, start, (acts, cots))
    return totals[0], totals[1]
```

```python
import jax
import jax.numpy as jnp
from jax import lax
from jax.experimental import pallas as pl
from jax.experimental.pallas import tpu as pltpu
from jax.sharding import PartitionSpec as P

F32 = jnp.float32
BF16 = jnp.bfloat16
STEP_TOKENS = 16


def grads_kernel(act_ref, cot_ref, left_ref, left_t_ref, right_ref, lower_ref, upper_ref, gl_ref, gr_ref):
    @pl.when(pl.program_id(0) == 0)
    def _():
        gl_ref[...] = jnp.zeros_like(gl_ref)
        gr_ref[...] = jnp.zeros_like(gr_ref)

    tokens = act_ref.shape[1]
    act = jnp.concatenate([act_ref[:, t].reshape(128, 128) for t in range(tokens)], axis=0)
    rot = jnp.dot(act, right_ref[...], preferred_element_type=F32).astype(BF16)
    rot = jnp.concatenate([rot[t * 128 : (t + 1) * 128] for t in range(tokens)], axis=1)
    trans = jnp.dot(left_t_ref[...], rot, preferred_element_type=F32)
    lower, upper = lower_ref[...], upper_ref[...]
    mids = []
    for t in range(tokens):
        tr = trans[:, t * 128 : (t + 1) * 128]
        cot = cot_ref[:, t].reshape(128, 128).astype(F32)
        mids.append(jnp.where((tr >= lower) & (tr <= upper), cot, 0.0).astype(BF16))
    mid = jnp.concatenate(mids, axis=1)
    back = jnp.dot(left_ref[...], mid, preferred_element_type=F32).astype(BF16)
    gl_ref[...] += lax.dot_general(rot, mid, (((1,), (1,)), ((), ())), preferred_element_type=F32)
    back = jnp.concatenate([back[:, t * 128 : (t + 1) * 128] for t in range(tokens)], axis=0)
    gr_ref[...] += lax.dot_general(act, back, (((0,), (0,)), ((), ())), preferred_element_type=F32)


def local_grads(act, cot, left, left_t, right, lower, upper):
    tokens = act.shape[1]
    whole = pl.BlockSpec((128, 128), lambda s: (0, 0))
    block = pl.BlockSpec((8, STEP_TOKENS, 16, 128), lambda s: (0, s, 0, 0))
    return pl.pallas_call(
        grads_kernel,
        grid=(tokens // STEP_TOKENS,),
        in_specs=[block, block] + [whole] * 5,
        out_specs=[whole, whole],
        out_shape=[jax.ShapeDtypeStruct((128, 128), F32)] * 2,
        compiler_params=pltpu.CompilerParams(vmem_limit_bytes=48 * 2**20),
        cost_estimate=pl.CostEstimate(flops=10 * tokens * 128**3, bytes_accessed=tokens * 2**16, transcendentals=0),
    )(act, cot, left, left_t, right, lower, upper)


def tensor_shift(y, core):
    return [(i, ((i // 2 + y) % 4) * 2 + ((i % 2) ^ core)) for i in range(8)]


def x_shift(s):
    return [(i, (i // 4) * 4 + (i % 4 + s) % 4) for i in range(32)]


def z_flip(b):
    return [(i, ((i // 4) ^ b) * 4 + i % 4) for i in range(32)]


def add_pair(x, axis, perm):
    return x + lax.ppermute(x, axis, perm)


def add_four(x, axis, shift):
    one, two, three = (lax.ppermute(x, axis, shift(s)) for s in (1, 2, 3))
    return (x + two) + (one + three)


def sum_all(grad_left, grad_right):
    core = lax.axis_index("tensor") % 2
    first = core == 0
    keep = jnp.where(first, grad_left, grad_right)
    give = jnp.where(first, grad_right, grad_left)
    swap = tensor_shift(0, 1)
    x = keep + lax.ppermute(give, "tensor", swap)
    x = add_four(x, "tensor", lambda s: tensor_shift(s, 0))
    x = add_four(x, "dp", x_shift)
    for b in (1, 2, 4):
        x = add_pair(x, "dp", z_flip(b))
    other = lax.ppermute(x, "tensor", swap)
    return jnp.where(first, x, other), jnp.where(first, other, x)


def exchange(x):
    return lax.all_to_all(x.reshape(8, -1, 16, 128), "tensor", 0, 0, tiled=False)


def on_device(activations, cotangent, left_factor, right_factor, scale_power, grid_bits):
    act, cot = exchange(activations), exchange(cotangent)
    step_size = jnp.exp2(scale_power.astype(F32))
    half_grid = jnp.exp2((grid_bits - 1).astype(F32))
    lower = -half_grid * step_size
    upper = (half_grid - 1.0) * step_size
    grad_left, grad_right = local_grads(
        act, cot, left_factor, left_factor.T, right_factor, lower, upper
    )
    return sum_all(grad_left, grad_right)


def solution(mesh):
    return jax.shard_map(
        on_device,
        mesh=mesh,
        in_specs=(P("dp", "tensor", None), P("dp", "tensor", None), P(), P(), P(), P()),
        out_specs=(P(), P()),
        check_vma=False,
    )
```

```python
import functools

import jax
import jax.numpy as jnp
from jax import lax
from jax.experimental import pallas as pl
from jax.experimental.pallas import tpu as pltpu
from jax.sharding import PartitionSpec as P

F32 = jnp.float32
BF16 = jnp.bfloat16
STEP_TOKENS = 8
ROWS = 16
PARTS = (32, 32)
WINDOW = 5
HOPS = ((1, 0), (3, 0), (2, 0), (2, 1), (0, 1), (1, 1), (3, 1))


def tensor_shift(y, core):
    return [(i, ((i // 2 + y) % 4) * 2 + ((i % 2) ^ core)) for i in range(8)]


def x_shift(s):
    return [(i, (i // 4) * 4 + (i % 4 + s) % 4) for i in range(32)]


def z_flip(b):
    return [(i, ((i // 4) ^ b) * 4 + i % 4) for i in range(32)]


def place():
    me = lax.axis_index("tensor")
    return me // 2, lax.rem(me, 2)


def peer(dy, dc):
    y, core = place()
    return lax.rem(y + dy + 4, 4) * 2 + (1 - core if dc else core)


def pack_kernel(first, hops, act_ref, cot_ref, *refs):
    outs, sems = refs[:-1], refs[-1]
    tokens = outs[0].shape[1]
    copies = []
    for k, (dy, dc) in enumerate(hops):
        for half, ref in enumerate((act_ref, cot_ref)):
            copies.append(
                pltpu.make_async_copy(
                    ref.at[peer(dy, dc), pl.ds(first, tokens)], outs[k].at[half], sems.at[2 * k + half]
                )
            )
    for copy in copies:
        copy.start()
    for copy in copies:
        copy.wait()


def pack(act, cot, first, tokens, hops):
    return pl.pallas_call(
        functools.partial(pack_kernel, first, hops),
        in_specs=[pl.BlockSpec(memory_space=pl.ANY)] * 2,
        out_specs=[pl.BlockSpec(memory_space=pltpu.VMEM)] * len(hops),
        out_shape=[jax.ShapeDtypeStruct((2, tokens, ROWS, 128), BF16)] * len(hops),
        scratch_shapes=[pltpu.SemaphoreType.DMA((2 * len(hops),))],
        cost_estimate=pl.CostEstimate(flops=0, bytes_accessed=len(hops) * tokens * 2**14, transcendentals=0),
        name="pack",
    )(act, cot)


def grads_kernel(*refs):
    parts, refs = refs[:8], refs[8:]
    (left_ref, left_t_ref, right_ref, lower_ref, upper_ref, gl_in, gr_in), refs = refs[:7], refs[7:]
    gl_ref, gr_ref, act_all, cot_all = refs
    left, left_t, right = left_ref[...], left_t_ref[...], right_ref[...]
    lower, upper = lower_ref[...], upper_ref[...]
    total = parts[0].shape[1]
    tokens = min(STEP_TOKENS, total)
    grad_left, grad_right = gl_in[...], gr_in[...]
    for k, (dy, dc) in enumerate(HOPS + ((0, 0),)):
        source = peer(-dy, dc)
        for t in range(total):
            rows = pl.ds(pl.multiple_of(t * 128 + source * ROWS, ROWS), ROWS)
            act_all[rows, :] = parts[k][0, t]
            cot_all[rows, :] = parts[k][1, t]
    for first in range(0, total, tokens):
        act = act_all[first * 128 : (first + tokens) * 128, :]
        rot = jnp.dot(act, right, preferred_element_type=F32).astype(BF16)
        rot = jnp.concatenate([rot[t * 128 : (t + 1) * 128] for t in range(tokens)], axis=1)
        trans = jnp.dot(left_t, rot, preferred_element_type=F32)
        mids = []
        for t in range(tokens):
            tr = trans[:, t * 128 : (t + 1) * 128]
            cot = cot_all[(first + t) * 128 : (first + t + 1) * 128, :].astype(F32)
            mids.append(jnp.where((tr >= lower) & (tr <= upper), cot, 0.0).astype(BF16))
        mid = jnp.concatenate(mids, axis=1)
        back = jnp.dot(left, mid, preferred_element_type=F32).astype(BF16)
        grad_left += lax.dot_general(rot, mid, (((1,), (1,)), ((), ())), preferred_element_type=F32)
        back = jnp.concatenate([back[:, t * 128 : (t + 1) * 128] for t in range(tokens)], axis=0)
        grad_right += lax.dot_general(act, back, (((0,), (0,)), ((), ())), preferred_element_type=F32)
    gl_ref[...] = grad_left
    gr_ref[...] = grad_right


def local_grads(parts, *rest):
    tokens = parts[0].shape[1]
    return pl.pallas_call(
        grads_kernel,
        in_specs=[pl.BlockSpec(memory_space=pltpu.VMEM)] * 15,
        out_specs=[pl.BlockSpec(memory_space=pltpu.VMEM)] * 2,
        out_shape=[jax.ShapeDtypeStruct((128, 128), F32)] * 2,
        scratch_shapes=[pltpu.VMEM((tokens * 128, 128), BF16)] * 2,
        compiler_params=pltpu.CompilerParams(vmem_limit_bytes=32 * 2**20),
        cost_estimate=pl.CostEstimate(flops=10 * tokens * 128**3, bytes_accessed=tokens * 2**16, transcendentals=0),
        name="grads",
    )(*parts, *rest)


def add_pair(x, axis, perm):
    return x + lax.ppermute(x, axis, perm)


def add_four(x, axis, shift):
    one, two, three = (lax.ppermute(x, axis, shift(s)) for s in (1, 2, 3))
    return (x + two) + (one + three)


def sum_all(grad_left, grad_right):
    core = lax.axis_index("tensor") % 2
    first = core == 0
    keep = jnp.where(first, grad_left, grad_right)
    give = jnp.where(first, grad_right, grad_left)
    swap = tensor_shift(0, 1)
    x = keep + lax.ppermute(give, "tensor", swap)
    x = add_four(x, "tensor", lambda s: tensor_shift(s, 0))
    x = add_four(x, "dp", x_shift)
    for b in (1, 2, 4):
        x = add_pair(x, "dp", z_flip(b))
    other = lax.ppermute(x, "tensor", swap)
    return jnp.where(first, x, other), jnp.where(first, other, x)


def exchange(act, cot):
    plan, first = [], 0
    for p, tokens in enumerate(PARTS):
        plan += [(p, first, tokens, hop) for hop in HOPS + ((0, 0),)]
        first += tokens
    lead = pack(act, cot, 0, PARTS[0], tuple(h for _, _, _, h in plan[:WINDOW]))
    act, cot, *lead = lax.optimization_barrier((act, cot, *lead))
    blocks = list(lead)
    blocks += pack(act, cot, 0, PARTS[0], (HOPS + ((0, 0),))[WINDOW:])
    first = PARTS[0]
    for tokens in PARTS[1:]:
        blocks += pack(act, cot, first, tokens, HOPS + ((0, 0),))
        first += tokens
    got, sent = [], []
    for (p, _, _, (dy, dc)), block in zip(plan, blocks):
        if (dy, dc) != (0, 0):
            if len(sent) >= WINDOW:
                w = sent[-WINDOW]
                block, got[w] = lax.optimization_barrier((block, got[w]))
            block = lax.ppermute(block, "tensor", tensor_shift(dy, dc))
            sent.append(len(got))
        got.append(block)
    return [got[8 * p : 8 * p + 8] for p in range(len(PARTS))]


def on_device(activations, cotangent, left_factor, right_factor, scale_power, grid_bits):
    act, cot = (x.reshape(8, -1, ROWS, 128) for x in (activations, cotangent))
    step_size = jnp.exp2(scale_power.astype(F32))
    half_grid = jnp.exp2((grid_bits - 1).astype(F32))
    lower = -half_grid * step_size
    upper = (half_grid - 1.0) * step_size
    grads = jnp.zeros((128, 128), F32), jnp.zeros((128, 128), F32)
    for part in exchange(act, cot):
        grads = local_grads(part, left_factor, left_factor.T, right_factor, lower, upper, *grads)
    return sum_all(*grads)


def solution(mesh):
    return jax.shard_map(
        on_device,
        mesh=mesh,
        in_specs=(P("dp", "tensor", None), P("dp", "tensor", None), P(), P(), P(), P()),
        out_specs=(P(), P()),
        check_vma=False,
    )
```

```python
import functools

import jax
import jax.numpy as jnp
from jax import lax
from jax.experimental import pallas as pl
from jax.experimental.pallas import tpu as pltpu
from jax.sharding import PartitionSpec as P

F32 = jnp.float32
BF16 = jnp.bfloat16
STEP_TOKENS = 8
ROWS = 16
PARTS = (32, 32)
WINDOW = 5
HOPS = (
    ((1, 0), (3, 0), (2, 0), (2, 1), (0, 1), (1, 1), (3, 1)),
    ((1, 0), (3, 0), (2, 0), (2, 1), (0, 1), (1, 1), (3, 1)),
)
OWN = ((0, 0),)


def tensor_shift(y, core):
    return [(i, ((i // 2 + y) % 4) * 2 + ((i % 2) ^ core)) for i in range(8)]


def place():
    me = lax.axis_index("tensor")
    return me // 2, lax.rem(me, 2)


def peer(dy, dc):
    y, core = place()
    return lax.rem(y + dy + 4, 4) * 2 + (1 - core if dc else core)


def pack_kernel(first, hops, act_ref, cot_ref, *refs):
    outs, sems = refs[:-1], refs[-1]
    tokens = outs[0].shape[1]
    copies = []
    for k, (dy, dc) in enumerate(hops):
        for half, ref in enumerate((act_ref, cot_ref)):
            copies.append(
                pltpu.make_async_copy(
                    ref.at[peer(dy, dc), pl.ds(first, tokens)], outs[k].at[half], sems.at[2 * k + half]
                )
            )
    for copy in copies:
        copy.start()
    for copy in copies:
        copy.wait()


def pack(act, cot, first, tokens, hops):
    return pl.pallas_call(
        functools.partial(pack_kernel, first, hops),
        in_specs=[pl.BlockSpec(memory_space=pl.ANY)] * 2,
        out_specs=[pl.BlockSpec(memory_space=pltpu.VMEM)] * len(hops),
        out_shape=[jax.ShapeDtypeStruct((2, tokens, ROWS, 128), BF16)] * len(hops),
        scratch_shapes=[pltpu.SemaphoreType.DMA((2 * len(hops),))],
        cost_estimate=pl.CostEstimate(flops=0, bytes_accessed=len(hops) * tokens * 2**14, transcendentals=0),
        name="pack",
    )(act, cot)


def grads_kernel(hops, *refs):
    parts, refs = refs[:8], refs[8:]
    (left_ref, left_t_ref, right_ref, lower_ref, upper_ref, gl_in, gr_in), refs = refs[:7], refs[7:]
    gl_ref, gr_ref, act_all, cot_all = refs
    left, left_t, right = left_ref[...], left_t_ref[...], right_ref[...]
    lower, upper = lower_ref[...], upper_ref[...]
    total = parts[0].shape[1]
    tokens = min(STEP_TOKENS, total)
    grad_left, grad_right = gl_in[...], gr_in[...]
    for k, (dy, dc) in enumerate(hops + OWN):
        source = peer(-dy, dc)
        for t in range(total):
            rows = pl.ds(pl.multiple_of(t * 128 + source * ROWS, ROWS), ROWS)
            act_all[rows, :] = parts[k][0, t]
            cot_all[rows, :] = parts[k][1, t]
    for first in range(0, total, tokens):
        act = act_all[first * 128 : (first + tokens) * 128, :]
        rot = jnp.dot(act, right, preferred_element_type=F32).astype(BF16)
        rot = jnp.concatenate([rot[t * 128 : (t + 1) * 128] for t in range(tokens)], axis=1)
        trans = jnp.dot(left_t, rot, preferred_element_type=F32)
        mids = []
        for t in range(tokens):
            tr = trans[:, t * 128 : (t + 1) * 128]
            cot = cot_all[(first + t) * 128 : (first + t + 1) * 128, :].astype(F32)
            mids.append(jnp.where((tr >= lower) & (tr <= upper), cot, 0.0).astype(BF16))
        mid = jnp.concatenate(mids, axis=1)
        back = jnp.dot(left, mid, preferred_element_type=F32).astype(BF16)
        grad_left += lax.dot_general(rot, mid, (((1,), (1,)), ((), ())), preferred_element_type=F32)
        back = jnp.concatenate([back[:, t * 128 : (t + 1) * 128] for t in range(tokens)], axis=0)
        grad_right += lax.dot_general(act, back, (((0,), (0,)), ((), ())), preferred_element_type=F32)
    gl_ref[...] = grad_left
    gr_ref[...] = grad_right


def local_grads(hops, parts, *rest):
    tokens = parts[0].shape[1]
    return pl.pallas_call(
        functools.partial(grads_kernel, hops),
        in_specs=[pl.BlockSpec(memory_space=pltpu.VMEM)] * 15,
        out_specs=[pl.BlockSpec(memory_space=pltpu.VMEM)] * 2,
        out_shape=[jax.ShapeDtypeStruct((128, 128), F32)] * 2,
        scratch_shapes=[pltpu.VMEM((tokens * 128, 128), BF16)] * 2,
        compiler_params=pltpu.CompilerParams(vmem_limit_bytes=32 * 2**20),
        cost_estimate=pl.CostEstimate(flops=10 * tokens * 128**3, bytes_accessed=tokens * 2**16, transcendentals=0),
        name="grads",
    )(*parts, *rest)


ALL = ("dp", "tensor")


ACROSS = (6, 7, 4, 5, 2, 3, 0, 1)


def along(axis, s):
    if axis == "y":
        return lambda z, x, y: (z, x, (y + s) % 4)
    if axis == "x":
        return lambda z, x, y: (z, (x + s) % 4, y)
    if axis == "z":
        return lambda z, x, y: (z // 4 * 4 + (z + s) % 4, x, y)
    return lambda z, x, y: (ACROSS[z], x, y)


def route(axes, s):
    pairs = []
    for i in range(256):
        z, x, y, core = i // 32, i // 8 % 4, i // 2 % 4, i % 2
        z, x, y = along(axes[core], s)(z, x, y)
        pairs.append((i, ((z * 4 + x) * 4 + y) * 2 + core))
    return pairs


def add_four(x, axes):
    one, two, three = (lax.ppermute(x, ALL, route(axes, s)) for s in (1, 2, 3))
    return (x + two) + (one + three)


def sum_all(grad_left, grad_right):
    core = lax.axis_index("tensor") % 2
    first = core == 0
    keep = jnp.where(first, grad_left, grad_right)
    give = jnp.where(first, grad_right, grad_left)
    swap = tensor_shift(0, 1)
    x = keep + lax.ppermute(give, "tensor", swap)
    x = add_four(x, "yx")
    x = add_four(x, "xy")
    x = add_four(x, "zz")
    x = x + lax.ppermute(x, ALL, route("hh", 1))
    other = lax.ppermute(x, "tensor", swap)
    return jnp.where(first, x, other), jnp.where(first, other, x)


def exchange(act, cot):
    plan, first = [], []
    for p, tokens in enumerate(PARTS):
        plan += [(p, hop) for hop in HOPS[p] + OWN]
        first.append(sum(PARTS[:p]))
    lead = pack(act, cot, 0, PARTS[0], HOPS[0][:WINDOW])
    act, cot, *lead = lax.optimization_barrier((act, cot, *lead))
    blocks = list(lead)
    blocks += pack(act, cot, 0, PARTS[0], HOPS[0][WINDOW:] + OWN)
    for p in range(1, len(PARTS)):
        blocks += pack(act, cot, first[p], PARTS[p], HOPS[p] + OWN)
    got, sent = [], []
    for (p, (dy, dc)), block in zip(plan, blocks):
        if (dy, dc) != (0, 0):
            if len(sent) >= WINDOW:
                w = sent[-WINDOW]
                block, got[w] = lax.optimization_barrier((block, got[w]))
            block = lax.ppermute(block, "tensor", tensor_shift(dy, dc))
            sent.append(len(got))
        got.append(block)
    return [got[8 * p : 8 * p + 8] for p in range(len(PARTS))]


def on_device(activations, cotangent, left_factor, right_factor, scale_power, grid_bits):
    act, cot = (x.reshape(8, -1, ROWS, 128) for x in (activations, cotangent))
    step_size = jnp.exp2(scale_power.astype(F32))
    half_grid = jnp.exp2((grid_bits - 1).astype(F32))
    lower = -half_grid * step_size
    upper = (half_grid - 1.0) * step_size
    grads = jnp.zeros((128, 128), F32), jnp.zeros((128, 128), F32)
    for hops, part in zip(HOPS, exchange(act, cot)):
        grads = local_grads(hops, part, left_factor, left_factor.T, right_factor, lower, upper, *grads)
    return sum_all(*grads)


def solution(mesh):
    return jax.shard_map(
        on_device,
        mesh=mesh,
        in_specs=(P("dp", "tensor", None), P("dp", "tensor", None), P(), P(), P(), P()),
        out_specs=(P(), P()),
        check_vma=False,
    )
```

```python
import functools

import jax
import jax.numpy as jnp
from jax import lax
from jax.experimental import pallas as pl
from jax.experimental.pallas import tpu as pltpu
from jax.sharding import PartitionSpec as P

F32 = jnp.float32
BF16 = jnp.bfloat16
STEP_TOKENS = 8
ROWS = 16
PARTS = (32, 32)
WINDOW = 5
HOPS = (
    ((1, 0), (3, 0), (2, 0), (2, 1), (0, 1), (1, 1), (3, 1)),
    ((1, 0), (3, 0), (2, 0), (2, 1), (0, 1), (1, 1), (3, 1)),
)
OWN = ((0, 0),)


def tensor_shift(y, core):
    return [(i, ((i // 2 + y) % 4) * 2 + ((i % 2) ^ core)) for i in range(8)]


def place():
    me = lax.axis_index("tensor")
    return me // 2, lax.rem(me, 2)


def peer(dy, dc):
    y, core = place()
    return lax.rem(y + dy + 4, 4) * 2 + (1 - core if dc else core)


def pack_kernel(first, hops, act_ref, cot_ref, *refs):
    outs, sems = refs[:-1], refs[-1]
    tokens = outs[0].shape[1]
    copies = []
    for k, (dy, dc) in enumerate(hops):
        for half, ref in enumerate((act_ref, cot_ref)):
            copies.append(
                pltpu.make_async_copy(
                    ref.at[peer(dy, dc), pl.ds(first, tokens)], outs[k].at[half], sems.at[2 * k + half]
                )
            )
    for copy in copies:
        copy.start()
    for copy in copies:
        copy.wait()


def pack(act, cot, first, tokens, hops):
    return pl.pallas_call(
        functools.partial(pack_kernel, first, hops),
        in_specs=[pl.BlockSpec(memory_space=pl.ANY)] * 2,
        out_specs=[pl.BlockSpec(memory_space=pltpu.VMEM)] * len(hops),
        out_shape=[jax.ShapeDtypeStruct((2, tokens, ROWS, 128), BF16)] * len(hops),
        scratch_shapes=[pltpu.SemaphoreType.DMA((2 * len(hops),))],
        cost_estimate=pl.CostEstimate(flops=0, bytes_accessed=len(hops) * tokens * 2**14, transcendentals=0),
        name="pack",
    )(act, cot)


def grads_kernel(hops, *refs):
    parts, refs = refs[:8], refs[8:]
    (left_ref, left_t_ref, right_ref, lower_ref, upper_ref, gl_in, gr_in), refs = refs[:7], refs[7:]
    gl_ref, gr_ref, act_all, cot_all = refs
    left, left_t, right = left_ref[...], left_t_ref[...], right_ref[...]
    lower, upper = lower_ref[...], upper_ref[...]
    total = parts[0].shape[1]
    tokens = min(STEP_TOKENS, total)
    grad_left, grad_right = gl_in[...], gr_in[...]
    for k, (dy, dc) in enumerate(hops + OWN):
        source = peer(-dy, dc)
        for t in range(total):
            rows = pl.ds(pl.multiple_of(t * 128 + source * ROWS, ROWS), ROWS)
            act_all[rows, :] = parts[k][0, t]
            cot_all[rows, :] = parts[k][1, t]
    for first in range(0, total, tokens):
        act = act_all[first * 128 : (first + tokens) * 128, :]
        rot = jnp.dot(act, right, preferred_element_type=F32).astype(BF16)
        rot = jnp.concatenate([rot[t * 128 : (t + 1) * 128] for t in range(tokens)], axis=1)
        trans = jnp.dot(left_t, rot, preferred_element_type=F32)
        mids = []
        for t in range(tokens):
            tr = trans[:, t * 128 : (t + 1) * 128]
            cot = cot_all[(first + t) * 128 : (first + t + 1) * 128, :].astype(F32)
            mids.append(jnp.where((tr >= lower) & (tr <= upper), cot, 0.0).astype(BF16))
        mid = jnp.concatenate(mids, axis=1)
        back = jnp.dot(left, mid, preferred_element_type=F32).astype(BF16)
        grad_left += lax.dot_general(rot, mid, (((1,), (1,)), ((), ())), preferred_element_type=F32)
        back = jnp.concatenate([back[:, t * 128 : (t + 1) * 128] for t in range(tokens)], axis=0)
        grad_right += lax.dot_general(act, back, (((0,), (0,)), ((), ())), preferred_element_type=F32)
    gl_ref[...] = grad_left
    gr_ref[...] = grad_right


def local_grads(hops, parts, *rest):
    tokens = parts[0].shape[1]
    return pl.pallas_call(
        functools.partial(grads_kernel, hops),
        in_specs=[pl.BlockSpec(memory_space=pltpu.VMEM)] * 15,
        out_specs=[pl.BlockSpec(memory_space=pltpu.VMEM)] * 2,
        out_shape=[jax.ShapeDtypeStruct((128, 128), F32)] * 2,
        scratch_shapes=[pltpu.VMEM((tokens * 128, 128), BF16)] * 2,
        compiler_params=pltpu.CompilerParams(vmem_limit_bytes=32 * 2**20),
        cost_estimate=pl.CostEstimate(flops=10 * tokens * 128**3, bytes_accessed=tokens * 2**16, transcendentals=0),
        name="grads",
    )(*parts, *rest)


ALL = ("dp", "tensor")


ACROSS = (6, 7, 4, 5, 2, 3, 0, 1)


def along(axis, s):
    if axis == "y":
        return lambda z, x, y: (z, x, (y + s) % 4)
    if axis == "x":
        return lambda z, x, y: (z, (x + s) % 4, y)
    if axis == "z":
        return lambda z, x, y: (z // 4 * 4 + (z + s) % 4, x, y)
    return lambda z, x, y: (ACROSS[z], x, y)


def route(axes, s):
    pairs = []
    for i in range(256):
        z, x, y, core = i // 32, i // 8 % 4, i // 2 % 4, i % 2
        z, x, y = along(axes[core], s)(z, x, y)
        pairs.append((i, ((z * 4 + x) * 4 + y) * 2 + core))
    return pairs


def add_four(x, axes):
    x = x.astype(BF16)
    x, one, two, three = (y.astype(F32) for y in [x] + [lax.ppermute(x, ALL, route(axes, s)) for s in (1, 2, 3)])
    return (x + two) + (one + three)


def sum_all(grad_left, grad_right):
    core = lax.axis_index("tensor") % 2
    first = core == 0
    keep = jnp.where(first, grad_left, grad_right)
    give = jnp.where(first, grad_right, grad_left)
    swap = tensor_shift(0, 1)
    x = keep + lax.ppermute(give, "tensor", swap)
    x = add_four(x, "yx")
    x = add_four(x, "xy")
    x = add_four(x, "zz")
    x = x + lax.ppermute(x, ALL, route("hh", 1))
    other = lax.ppermute(x, "tensor", swap)
    return jnp.where(first, x, other), jnp.where(first, other, x)


def exchange(act, cot):
    plan, first = [], []
    for p, tokens in enumerate(PARTS):
        plan += [(p, hop) for hop in HOPS[p] + OWN]
        first.append(sum(PARTS[:p]))
    lead = pack(act, cot, 0, PARTS[0], HOPS[0][:WINDOW])
    act, cot, *lead = lax.optimization_barrier((act, cot, *lead))
    blocks = list(lead)
    blocks += pack(act, cot, 0, PARTS[0], HOPS[0][WINDOW:] + OWN)
    for p in range(1, len(PARTS)):
        blocks += pack(act, cot, first[p], PARTS[p], HOPS[p] + OWN)
    got, sent = [], []
    for (p, (dy, dc)), block in zip(plan, blocks):
        if (dy, dc) != (0, 0):
            if len(sent) >= WINDOW:
                w = sent[-WINDOW]
                block, got[w] = lax.optimization_barrier((block, got[w]))
            block = lax.ppermute(block, "tensor", tensor_shift(dy, dc))
            sent.append(len(got))
        got.append(block)
    return [got[8 * p : 8 * p + 8] for p in range(len(PARTS))]


def on_device(activations, cotangent, left_factor, right_factor, scale_power, grid_bits):
    act, cot = (x.reshape(8, -1, ROWS, 128) for x in (activations, cotangent))
    step_size = jnp.exp2(scale_power.astype(F32))
    half_grid = jnp.exp2((grid_bits - 1).astype(F32))
    lower = -half_grid * step_size
    upper = (half_grid - 1.0) * step_size
    grads = jnp.zeros((128, 128), F32), jnp.zeros((128, 128), F32)
    for hops, part in zip(HOPS, exchange(act, cot)):
        grads = local_grads(hops, part, left_factor, left_factor.T, right_factor, lower, upper, *grads)
    return sum_all(*grads)


def solution(mesh):
    return jax.shard_map(
        on_device,
        mesh=mesh,
        in_specs=(P("dp", "tensor", None), P("dp", "tensor", None), P(), P(), P(), P()),
        out_specs=(P(), P()),
        check_vma=False,
    )
```

```python
import functools

import jax
import jax.numpy as jnp
from jax import lax
from jax.experimental import pallas as pl
from jax.experimental.pallas import tpu as pltpu
from jax.sharding import PartitionSpec as P

F32 = jnp.float32
BF16 = jnp.bfloat16
STEP_TOKENS = 16
ROWS = 16
PARTS = (32, 32)
WINDOW = 5
HOPS = (
    ((1, 0), (3, 0), (2, 0), (2, 1), (0, 1), (1, 1), (3, 1)),
    ((1, 0), (3, 0), (2, 0), (2, 1), (0, 1), (1, 1), (3, 1)),
)
OWN = ((0, 0),)


def tensor_shift(y, core):
    return [(i, ((i // 2 + y) % 4) * 2 + ((i % 2) ^ core)) for i in range(8)]


def place():
    me = lax.axis_index("tensor")
    return me // 2, lax.rem(me, 2)


def peer(dy, dc):
    y, core = place()
    return lax.rem(y + dy + 4, 4) * 2 + (1 - core if dc else core)


def pack_kernel(first, hops, act_ref, cot_ref, *refs):
    outs, sems = refs[:-1], refs[-1]
    tokens = outs[0].shape[1]
    copies = []
    for k, (dy, dc) in enumerate(hops):
        for half, ref in enumerate((act_ref, cot_ref)):
            copies.append(
                pltpu.make_async_copy(
                    ref.at[peer(dy, dc), pl.ds(first, tokens)], outs[k].at[half], sems.at[2 * k + half]
                )
            )
    for copy in copies:
        copy.start()
    for copy in copies:
        copy.wait()


def pack(act, cot, first, tokens, hops):
    return pl.pallas_call(
        functools.partial(pack_kernel, first, hops),
        in_specs=[pl.BlockSpec(memory_space=pl.ANY)] * 2,
        out_specs=[pl.BlockSpec(memory_space=pltpu.VMEM)] * len(hops),
        out_shape=[jax.ShapeDtypeStruct((2, tokens, ROWS, 128), BF16)] * len(hops),
        scratch_shapes=[pltpu.SemaphoreType.DMA((2 * len(hops),))],
        cost_estimate=pl.CostEstimate(flops=0, bytes_accessed=len(hops) * tokens * 2**14, transcendentals=0),
        name="pack",
    )(act, cot)


def grads_kernel(hops, *refs):
    parts, refs = refs[:8], refs[8:]
    (left_ref, left_t_ref, right_ref, lower_ref, upper_ref, gl_in, gr_in), refs = refs[:7], refs[7:]
    gl_ref, gr_ref, act_all, cot_all = refs
    left, left_t, right = left_ref[...], left_t_ref[...], right_ref[...]
    lower, upper = lower_ref[...], upper_ref[...]
    total = parts[0].shape[1]
    tokens = min(STEP_TOKENS, total)
    grad_left, grad_right = gl_in[...], gr_in[...]
    sources = [peer(-dy, dc) * ROWS for dy, dc in hops + OWN]
    for first in range(0, total, tokens):
        for k, source in enumerate(sources):
            for t in range(first, first + tokens):
                rows = pl.ds(pl.multiple_of(t * 128 + source, ROWS), ROWS)
                act_all[rows, :] = parts[k][0, t]
                cot_all[rows, :] = parts[k][1, t]
        act = act_all[first * 128 : (first + tokens) * 128, :]
        rot = jnp.dot(act, right, preferred_element_type=F32).astype(BF16)
        rot = jnp.concatenate([rot[t * 128 : (t + 1) * 128] for t in range(tokens)], axis=1)
        trans = jnp.dot(left_t, rot, preferred_element_type=F32)
        mids = []
        for t in range(tokens):
            tr = trans[:, t * 128 : (t + 1) * 128]
            cot = cot_all[(first + t) * 128 : (first + t + 1) * 128, :].astype(F32)
            mids.append(jnp.where((tr >= lower) & (tr <= upper), cot, 0.0).astype(BF16))
        mid = jnp.concatenate(mids, axis=1)
        back = jnp.dot(left, mid, preferred_element_type=F32).astype(BF16)
        grad_left += lax.dot_general(rot, mid, (((1,), (1,)), ((), ())), preferred_element_type=F32)
        back = jnp.concatenate([back[:, t * 128 : (t + 1) * 128] for t in range(tokens)], axis=0)
        grad_right += lax.dot_general(act, back, (((0,), (0,)), ((), ())), preferred_element_type=F32)
    gl_ref[...] = grad_left
    gr_ref[...] = grad_right


def local_grads(hops, parts, *rest):
    tokens = parts[0].shape[1]
    return pl.pallas_call(
        functools.partial(grads_kernel, hops),
        in_specs=[pl.BlockSpec(memory_space=pltpu.VMEM)] * 15,
        out_specs=[pl.BlockSpec(memory_space=pltpu.VMEM)] * 2,
        out_shape=[jax.ShapeDtypeStruct((128, 128), F32)] * 2,
        scratch_shapes=[pltpu.VMEM((tokens * 128, 128), BF16)] * 2,
        compiler_params=pltpu.CompilerParams(vmem_limit_bytes=32 * 2**20),
        cost_estimate=pl.CostEstimate(flops=10 * tokens * 128**3, bytes_accessed=tokens * 2**16, transcendentals=0),
        name="grads",
    )(*parts, *rest)


ALL = ("dp", "tensor")


ACROSS = (6, 7, 4, 5, 2, 3, 0, 1)


def along(axis, s):
    if axis == "y":
        return lambda z, x, y: (z, x, (y + s) % 4)
    if axis == "x":
        return lambda z, x, y: (z, (x + s) % 4, y)
    if axis == "z":
        return lambda z, x, y: (z // 4 * 4 + (z + s) % 4, x, y)
    return lambda z, x, y: (ACROSS[z], x, y)


def route(axes, s):
    pairs = []
    for i in range(256):
        z, x, y, core = i // 32, i // 8 % 4, i // 2 % 4, i % 2
        z, x, y = along(axes[core], s)(z, x, y)
        pairs.append((i, ((z * 4 + x) * 4 + y) * 2 + core))
    return pairs


def add_four(x, axes):
    x = x.astype(BF16)
    x, one, two, three = (y.astype(F32) for y in [x] + [lax.ppermute(x, ALL, route(axes, s)) for s in (1, 2, 3)])
    return (x + two) + (one + three)


def sum_all(grad_left, grad_right):
    core = lax.axis_index("tensor") % 2
    first = core == 0
    keep = jnp.where(first, grad_left, grad_right)
    give = jnp.where(first, grad_right, grad_left)
    swap = tensor_shift(0, 1)
    x = keep + lax.ppermute(give, "tensor", swap)
    x = add_four(x, "yx")
    x = add_four(x, "xy")
    x = add_four(x, "zz")
    x = x + lax.ppermute(x, ALL, route("hh", 1))
    other = lax.ppermute(x, "tensor", swap)
    return jnp.where(first, x, other), jnp.where(first, other, x)


def exchange(act, cot):
    plan, first = [], []
    for p, tokens in enumerate(PARTS):
        plan += [(p, hop) for hop in HOPS[p] + OWN]
        first.append(sum(PARTS[:p]))
    lead = pack(act, cot, 0, PARTS[0], HOPS[0][:WINDOW])
    act, cot, *lead = lax.optimization_barrier((act, cot, *lead))
    blocks = list(lead)
    blocks += pack(act, cot, 0, PARTS[0], HOPS[0][WINDOW:] + OWN)
    for p in range(1, len(PARTS)):
        blocks += pack(act, cot, first[p], PARTS[p], HOPS[p] + OWN)
    got, sent = [], []
    for (p, (dy, dc)), block in zip(plan, blocks):
        if (dy, dc) != (0, 0):
            if len(sent) >= WINDOW:
                w = sent[-WINDOW]
                block, got[w] = lax.optimization_barrier((block, got[w]))
            block = lax.ppermute(block, "tensor", tensor_shift(dy, dc))
            sent.append(len(got))
        got.append(block)
    return [got[8 * p : 8 * p + 8] for p in range(len(PARTS))]


def on_device(activations, cotangent, left_factor, right_factor, scale_power, grid_bits):
    act, cot = (x.reshape(8, -1, ROWS, 128) for x in (activations, cotangent))
    step_size = jnp.exp2(scale_power.astype(F32))
    half_grid = jnp.exp2((grid_bits - 1).astype(F32))
    lower = -half_grid * step_size
    upper = (half_grid - 1.0) * step_size
    grads = jnp.zeros((128, 128), F32), jnp.zeros((128, 128), F32)
    for hops, part in zip(HOPS, exchange(act, cot)):
        grads = local_grads(hops, part, left_factor, left_factor.T, right_factor, lower, upper, *grads)
    return sum_all(*grads)


def solution(mesh):
    return jax.shard_map(
        on_device,
        mesh=mesh,
        in_specs=(P("dp", "tensor", None), P("dp", "tensor", None), P(), P(), P(), P()),
        out_specs=(P(), P()),
        check_vma=False,
    )
```

```python
import functools

import jax
import jax.numpy as jnp
from jax import lax
from jax.experimental import pallas as pl
from jax.experimental.pallas import tpu as pltpu
from jax.sharding import PartitionSpec as P

F32 = jnp.float32
BF16 = jnp.bfloat16
STEP_TOKENS = 16
ROWS = 16
PARTS = (32, 32)
WINDOW = 5
HOPS = (
    ((1, 0), (3, 0), (2, 0), (2, 1), (0, 1), (1, 1), (3, 1)),
    ((1, 0), (3, 0), (2, 0), (2, 1), (0, 1), (1, 1), (3, 1)),
)
OWN = ((0, 0),)


def tensor_shift(y, core):
    return [(i, ((i // 2 + y) % 4) * 2 + ((i % 2) ^ core)) for i in range(8)]


def place():
    me = lax.axis_index("tensor")
    return me // 2, lax.rem(me, 2)


def peer(dy, dc):
    y, core = place()
    return lax.rem(y + dy + 4, 4) * 2 + (1 - core if dc else core)


def pack_kernel(first, hops, act_ref, cot_ref, *refs):
    outs, sems = refs[:-1], refs[-1]
    tokens = outs[0].shape[1]
    copies = []
    for k, (dy, dc) in enumerate(hops):
        for half, ref in enumerate((act_ref, cot_ref)):
            copies.append(
                pltpu.make_async_copy(
                    ref.at[peer(dy, dc), pl.ds(first, tokens)], outs[k].at[half], sems.at[2 * k + half]
                )
            )
    for copy in copies:
        copy.start()
    for copy in copies:
        copy.wait()


def pack(act, cot, first, tokens, hops):
    return pl.pallas_call(
        functools.partial(pack_kernel, first, hops),
        in_specs=[pl.BlockSpec(memory_space=pl.ANY)] * 2,
        out_specs=[pl.BlockSpec(memory_space=pltpu.VMEM)] * len(hops),
        out_shape=[jax.ShapeDtypeStruct((2, tokens, ROWS, 128), BF16)] * len(hops),
        scratch_shapes=[pltpu.SemaphoreType.DMA((2 * len(hops),))],
        cost_estimate=pl.CostEstimate(flops=0, bytes_accessed=len(hops) * tokens * 2**14, transcendentals=0),
        name="pack",
    )(act, cot)


def grads_kernel(hops, *refs):
    parts, refs = refs[:8], refs[8:]
    (left_ref, left_t_ref, right_ref, lower_ref, upper_ref, gl_in, gr_in), refs = refs[:7], refs[7:]
    gl_ref, gr_ref, act_all, cot_all = refs
    left, left_t, right = left_ref[...], left_t_ref[...], right_ref[...]
    lower, upper = lower_ref[...], upper_ref[...]
    total = parts[0].shape[1]
    tokens = min(STEP_TOKENS, total)
    grad_left, grad_right = gl_in[...], gr_in[...]
    sources = [peer(-dy, dc) * ROWS for dy, dc in hops + OWN]
    for first in range(0, total, tokens):
        for k, source in enumerate(sources):
            for t in range(first, first + tokens):
                rows = pl.ds(pl.multiple_of(t * 128 + source, ROWS), ROWS)
                act_all[rows, :] = parts[k][0, t]
                cot_all[rows, :] = parts[k][1, t]
        act = act_all[first * 128 : (first + tokens) * 128, :]
        rot = jnp.dot(act, right, preferred_element_type=F32).astype(BF16)
        rot = jnp.concatenate([rot[t * 128 : (t + 1) * 128] for t in range(tokens)], axis=1)
        trans = jnp.dot(left_t, rot, preferred_element_type=F32)
        mids = []
        for t in range(tokens):
            tr = trans[:, t * 128 : (t + 1) * 128]
            cot = cot_all[(first + t) * 128 : (first + t + 1) * 128, :].astype(F32)
            mids.append(jnp.where((tr >= lower) & (tr <= upper), cot, 0.0).astype(BF16))
        mid = jnp.concatenate(mids, axis=1)
        back = jnp.dot(left, mid, preferred_element_type=F32).astype(BF16)
        grad_left += lax.dot_general(rot, mid, (((1,), (1,)), ((), ())), preferred_element_type=F32)
        back = jnp.concatenate([back[:, t * 128 : (t + 1) * 128] for t in range(tokens)], axis=0)
        grad_right += lax.dot_general(act, back, (((0,), (0,)), ((), ())), preferred_element_type=F32)
    gl_ref[...] = grad_left
    gr_ref[...] = grad_right


def local_grads(hops, parts, *rest):
    tokens = parts[0].shape[1]
    return pl.pallas_call(
        functools.partial(grads_kernel, hops),
        in_specs=[pl.BlockSpec(memory_space=pltpu.VMEM)] * 15,
        out_specs=[pl.BlockSpec(memory_space=pltpu.VMEM)] * 2,
        out_shape=[jax.ShapeDtypeStruct((128, 128), F32)] * 2,
        scratch_shapes=[pltpu.VMEM((tokens * 128, 128), BF16)] * 2,
        compiler_params=pltpu.CompilerParams(vmem_limit_bytes=32 * 2**20),
        cost_estimate=pl.CostEstimate(flops=10 * tokens * 128**3, bytes_accessed=tokens * 2**16, transcendentals=0),
        name="grads",
    )(*parts, *rest)


ALL = ("dp", "tensor")


ACROSS = (6, 7, 4, 5, 2, 3, 0, 1)


def along(axis, s):
    if axis == "y":
        return lambda z, x, y: (z, x, (y + s) % 4)
    if axis == "x":
        return lambda z, x, y: (z, (x + s) % 4, y)
    if axis == "z":
        return lambda z, x, y: (z // 4 * 4 + (z + s) % 4, x, y)
    return lambda z, x, y: (ACROSS[z], x, y)


def route(axes, s):
    pairs = []
    for i in range(256):
        z, x, y, core = i // 32, i // 8 % 4, i // 2 % 4, i % 2
        z, x, y = along(axes[core], s)(z, x, y)
        pairs.append((i, ((z * 4 + x) * 4 + y) * 2 + core))
    return pairs


def add_four(x, axes):
    x = x.astype(BF16)
    x, one, two, three = (y.astype(F32) for y in [x] + [lax.ppermute(x, ALL, route(axes, s)) for s in (1, 2, 3)])
    return (x + two) + (one + three)


def sum_all(grad_left, grad_right):
    core = lax.axis_index("tensor") % 2
    first = core == 0
    keep = jnp.where(first, grad_left, grad_right)
    give = jnp.where(first, grad_right, grad_left)
    swap = tensor_shift(0, 1)
    x = keep + lax.ppermute(give, "tensor", swap)
    x = add_four(x, "zz")
    x = add_four(x, "yx")
    x = add_four(x, "xy")
    x = x.astype(BF16)
    x = x.astype(F32) + lax.ppermute(x, ALL, route("hh", 1)).astype(F32)
    other = lax.ppermute(x, "tensor", swap)
    return jnp.where(first, x, other), jnp.where(first, other, x)


def exchange(act, cot):
    plan, first = [], []
    for p, tokens in enumerate(PARTS):
        plan += [(p, hop) for hop in HOPS[p] + OWN]
        first.append(sum(PARTS[:p]))
    lead = pack(act, cot, 0, PARTS[0], HOPS[0][:WINDOW])
    act, cot, *lead = lax.optimization_barrier((act, cot, *lead))
    blocks = list(lead)
    blocks += pack(act, cot, 0, PARTS[0], HOPS[0][WINDOW:] + OWN)
    for p in range(1, len(PARTS)):
        blocks += pack(act, cot, first[p], PARTS[p], HOPS[p] + OWN)
    got, sent = [], []
    for (p, (dy, dc)), block in zip(plan, blocks):
        if (dy, dc) != (0, 0):
            if len(sent) >= WINDOW:
                w = sent[-WINDOW]
                block, got[w] = lax.optimization_barrier((block, got[w]))
            block = lax.ppermute(block, "tensor", tensor_shift(dy, dc))
            sent.append(len(got))
        got.append(block)
    return [got[8 * p : 8 * p + 8] for p in range(len(PARTS))]


def on_device(activations, cotangent, left_factor, right_factor, scale_power, grid_bits):
    act, cot = (x.reshape(8, -1, ROWS, 128) for x in (activations, cotangent))
    step_size = jnp.exp2(scale_power.astype(F32))
    half_grid = jnp.exp2((grid_bits - 1).astype(F32))
    lower = -half_grid * step_size
    upper = (half_grid - 1.0) * step_size
    grads = jnp.zeros((128, 128), F32), jnp.zeros((128, 128), F32)
    for hops, part in zip(HOPS, exchange(act, cot)):
        grads = local_grads(hops, part, left_factor, left_factor.T, right_factor, lower, upper, *grads)
    return sum_all(*grads)


def solution(mesh):
    return jax.shard_map(
        on_device,
        mesh=mesh,
        in_specs=(P("dp", "tensor", None), P("dp", "tensor", None), P(), P(), P(), P()),
        out_specs=(P(), P()),
        check_vma=False,
    )
```
